128 devices in a mesh: section: 4 (over z_hi, core), expert: 32 (over z_lo, x, y).
Axes of the slice: x: 4, y: 4, z: 4 (z_hi: 2, z_lo: 2; z = z_hi * 2 + z_lo), core: 2. Of those that a mesh axis runs over, the one named last changes fastest.
Arguments:
- activations: bfloat16 [4, 4096, 3584], P('section', 'expert'), may hold values from -21 to 21
- norm_gain: float32 [4, 3584], P('section'), may hold values from 0.1 to 1.9
- w_gate: bfloat16 [4, 32, 3584, 1024], P('section', 'expert'), may hold values from -0.09375 to 0.09375
- w_up: bfloat16 [4, 32, 3584, 1024], P('section', 'expert'), may hold values from -0.09375 to 0.09375
- w_down: bfloat16 [4, 32, 1024, 3584], P('section', 'expert'), may hold values from -0.1875 to 0.1875
- routes: int32 [2, 4, 4096, 2], P(None, 'section', 'expert'), may hold values from 0 to 31, all different within a row; in each aligned block of 128 rows (0 to 127, 128 to 255, ..., all dimensions but the last counted through in order) at most 16 rows name the same one
- gate_logits: float32 [2, 4, 4096, 2], P(None, 'section', 'expert'), may hold values from -6 to 6
Outputs:
- advanced: bfloat16 [4, 4096, 3584], P('section', 'expert')
The draws below stay inside these ranges and needn't reach their ends.
Inputs may be any that keep to these rules, and one draw needn't show every extreme that they name: `routes`: within each aligned block of 128 token rows (the rows of one device for one step and section) each row names 2 different experts and no expert is named by more than 16 rows; some expert is named by exactly 16 rows.
All inputs are finite; a program needn't handle non-finite values.
Results may differ from the reference program's by a relative error of at most 0.0057.
Values may be sent and summed in bfloat16 or wider, within the bound.
No kernel may reach another device: no remote copies, remote signals or barrier semaphores. Data moves between devices by JAX's collectives and lax.ppermute only.
A program may use at most 192 MiB of HBM per device.

```python
import math
import jax
import jax.numpy as jnp
import numpy as np
from jax import lax

D = 3584
FF = 1024
TOK_DEV = 128
TOP = 2
STEPS = 2
EXPERTS = 32
MB_TOK = 4096
CAP = 16
N_SECTION = 4
N_EXPERT = 32


def draw_activations(key, part):
    key = jax.random.fold_in(key, 11)
    base_key, row_key, column_key = jax.random.split(key, 3)
    shape = (N_SECTION, MB_TOK, D)
    base = jnp.clip(jax.random.normal(base_key, shape, jnp.float32), -4.0, 4.0)
    rows = jnp.exp(jax.random.uniform(row_key, (N_SECTION, MB_TOK, 1), jnp.float32, math.log(0.3), math.log(3.0)))
    columns = jnp.exp(jax.random.uniform(column_key, (D,), jnp.float32, math.log(0.6), math.log(1.7)))
    return (base * rows * columns).astype(jnp.bfloat16)


def levels(key, dims, cuts, smallest, high):
    def one(dim, parts):
        heights = jax.random.uniform(jax.random.fold_in(jax.random.fold_in(key, 6), dim), (parts,), jnp.float32, smallest / len(cuts), high / len(cuts))
        return jnp.repeat(jnp.exp(heights), dims[dim] // parts).reshape((-1,) + (1,) * (len(dims) - dim - 1))

    factor_of = one(*cuts[0])
    for cut in cuts[1:]:
        factor_of = factor_of * one(*cut)
    return factor_of


def deal_out(rng, own, number, rows, amount, top, reach, lean):
    sequence = jax.random.permutation(rng, amount)
    crowded, usual = load_shares(amount, rows * top, reach, lean, True), load_shares(amount, rows * top, reach, lean, False)
    places = jnp.arange(amount)

    def named(tallies, rotation):
        used = int((tallies > 0).sum())
        fixed = max(1, used // 4)
        moved = fixed + (places - fixed + rotation * (used - fixed)) % max(1, amount - fixed)
        return jnp.zeros((amount,), jnp.int32).at[sequence[jnp.where(places < fixed, places, moved)]].set(jnp.asarray(tallies, jnp.int32))

    tallies = jnp.where(number % 4 == 0, named(crowded, number // 4), named(usual, number - number // 4 - 1))
    mixed = jax.random.permutation(jax.random.fold_in(own, 3), amount)
    donor, receiver = mixed[0:amount // 2 * 2:2], mixed[1:amount // 2 * 2:2]
    margin = jnp.minimum(tallies[donor] - 1, reach - tallies[receiver]) // 2
    margin = jnp.where((donor == sequence[0]) | (receiver == sequence[0]) | (tallies[receiver] == 0), 0, jnp.maximum(margin, 0))
    moved = jax.random.randint(jax.random.fold_in(own, 4), (amount // 2,), 0, 1 << 20) % (margin + 1)
    tallies = tallies.at[donor].add(-moved).at[receiver].add(moved)
    members = jnp.searchsorted(jnp.cumsum(tallies), jnp.arange(rows * top), side="right").astype(jnp.int32)
    grid = members.reshape(top, rows).T
    grid = grid[jax.random.permutation(jax.random.fold_in(own, 1), rows)]
    rotation = jax.random.randint(jax.random.fold_in(own, 2), (rows, 1), 0, top)
    return jnp.take_along_axis(grid, (jnp.arange(top)[None, :] + rotation) % top, axis=1)


def load_shares(count, total, limit, lean, full):
    portions = [(1 << 20) // math.isqrt(standing ** lean) + 1 for standing in range(1, count + 1)]
    largest = limit if full else min(limit, max(-(-total // count), total * portions[0] // sum(portions)))
    least = 1 if total - largest >= count - 1 else 0
    holding, surplus = [largest] + [least] * (count - 1), total - largest - least * (count - 1)
    while surplus > 0:
        movable = [i for i in range(1, count) if holding[i] < largest] or [i for i in range(1, count) if holding[i] < limit]
        pool, remaining = sum([portions[i] for i in movable]), surplus
        for i in movable:
            extra = min(limit - holding[i], max(1, remaining * portions[i] // pool), surplus)
            holding[i] = holding[i] + extra
            surplus = surplus - extra
    return np.array(holding)


def normal_values(key, shape, spread, reach, cuts=(), kind=jnp.bfloat16):
    values = jax.random.normal(key, shape, jnp.float32) * spread
    if len(cuts) > 0:
        values = levels(key, shape, cuts, -0.22, 0.18) * values
    return jnp.clip(values, min=-reach, max=reach).astype(kind)


def setup_inputs(seed: int = 0) -> dict:
    keys = jax.random.split(jax.random.key(seed), 8)
    activations = draw_activations(jax.random.fold_in(keys[7], 71), 0)
    norm_gain = jnp.clip(1.0 + 0.18 * jax.random.normal(keys[1], (N_SECTION, D), jnp.float32), 0.1, 1.9)
    w_gate = normal_values(keys[2], (N_SECTION, EXPERTS, D, FF), D ** -0.5, 0.09375, ((0, 4), (1, 32)))
    w_up = normal_values(keys[3], (N_SECTION, EXPERTS, D, FF), D ** -0.5, 0.09375, ((0, 4), (1, 32)))
    w_down = normal_values(keys[4], (N_SECTION, EXPERTS, FF, D), FF ** -0.5, 0.1875, ((0, 4), (1, 32)))
    routes_keys = jax.random.split(jax.random.fold_in(keys[5], 1), STEPS * N_SECTION * MB_TOK // TOK_DEV)
    routes_turns = jax.random.permutation(jax.random.fold_in(keys[5], 3), STEPS * N_SECTION * MB_TOK // TOK_DEV)
    routes = jax.vmap(lambda own, number: deal_out(jax.random.fold_in(keys[5], 2), own, number, TOK_DEV, EXPERTS, TOP, CAP, 2))(routes_keys, routes_turns).reshape((STEPS, N_SECTION, MB_TOK, TOP))
    gate_logits = normal_values(keys[6], (STEPS, N_SECTION, MB_TOK, TOP), 1.5, 6.0, ((1, 4), (2, 32)), jnp.float32)
    return dict(activations=activations, norm_gain=norm_gain, w_gate=w_gate, w_up=w_up, w_down=w_down, routes=routes, gate_logits=gate_logits)


EPSILON = 1e-06

def normalize(values_in, gain):
    values = values_in.astype(jnp.float32)
    scaling = lax.rsqrt(lax.optimization_barrier(jnp.mean(values * values, axis=-1, keepdims=True)) + EPSILON)
    return (values * scaling * gain).astype(jnp.bfloat16)

def gate_share(logits):
    lifted = jax.nn.sigmoid(logits)
    return lifted / lax.optimization_barrier(jnp.sum(lifted, axis=-1, keepdims=True))

def slot_table(chosen, number_experts, capacity):
    token_count, choices = chosen.shape
    flattened = chosen.reshape(-1)
    indicator = (flattened[:, None] == jnp.arange(number_experts, dtype=jnp.int32)[None, :]).astype(jnp.int32)
    earlier = jnp.cumsum(indicator, axis=0) - indicator
    position = lax.optimization_barrier(jnp.sum(earlier * indicator, axis=1)).astype(jnp.int32)
    places = jnp.arange(capacity, dtype=jnp.int32)
    matches = (indicator.T[:, None, :] == 1) & (position[None, None, :] == places[None, :, None])
    owners = jnp.arange(token_count * choices, dtype=jnp.int32) // choices
    picked = lax.optimization_barrier(jnp.sum(jnp.where(matches, owners[None, None, :] + 1, 0), axis=2)).astype(jnp.int32) - 1
    picked = jnp.where(picked < 0, token_count, picked).astype(jnp.int32)
    return (position.reshape(token_count, choices), picked)

def expert_forward(rows, gate_matrix, up_matrix, down_matrix):
    gate = jnp.dot(rows, gate_matrix, preferred_element_type=jnp.float32)
    upward = jnp.dot(rows, up_matrix, preferred_element_type=jnp.float32)
    hidden = (jax.nn.silu(gate) * upward).astype(jnp.bfloat16)
    return jnp.dot(hidden, down_matrix, preferred_element_type=jnp.float32).astype(jnp.bfloat16)

def layer(values_in, gain, gate_all, up_all, down_all, chosen_all, logits_all):
    normed = normalize(values_in, gain).reshape(N_EXPERT, TOK_DEV, D)
    chosen = chosen_all.reshape(N_EXPERT, TOK_DEV, TOP)
    shares = gate_share(logits_all).reshape(N_EXPERT, TOK_DEV, TOP)
    slots, picks = jax.vmap(lambda lists: slot_table(lists, EXPERTS, CAP))(chosen)
    padded = jnp.concatenate([normed, jnp.zeros((N_EXPERT, 1, D), jnp.bfloat16)], axis=1)
    buffers = jax.vmap(lambda rows, index: rows[index])(padded, picks)
    buffers = jnp.transpose(buffers, (1, 0, 2, 3))

    def run_expert(packed):
        rows, gate_matrix, up_matrix, down_matrix = packed
        produced = expert_forward(rows.reshape(N_EXPERT * CAP, D), gate_matrix, up_matrix, down_matrix)
        return produced.reshape(N_EXPERT, CAP, D)
    produced = lax.map(run_expert, (buffers, gate_all, up_all, down_all))
    produced = jnp.transpose(produced, (1, 0, 2, 3))
    fetched = jax.vmap(lambda table, experts_of, slots_of: table[experts_of, slots_of])(produced, chosen, slots)
    mixed = lax.optimization_barrier(jnp.sum(shares[..., None] * fetched.astype(jnp.float32), axis=2))
    result = values_in.astype(jnp.float32).reshape(N_EXPERT, TOK_DEV, D) + mixed
    return result.astype(jnp.bfloat16).reshape(MB_TOK, D)

def reference(activations, norm_gain, w_gate, w_up, w_down, routes, gate_logits):
    current = activations
    for step_index in range(STEPS):
        results = [layer(current[section_index], norm_gain[section_index], w_gate[section_index], w_up[section_index], w_down[section_index], routes[step_index, section_index], gate_logits[step_index, section_index]) for section_index in range(N_SECTION)]
        current = jnp.roll(jnp.stack(results), 1, axis=0)
    return current
```

```python
import functools

import jax
import jax.numpy as jnp
from jax import lax
from jax.experimental import pallas as pl
from jax.experimental.pallas import tpu as pltpu
from jax.sharding import PartitionSpec as P

TOP = 2
STEPS = 2
EPSILON = 1e-06
VMEM_LIMIT = 56 * 1024 * 1024


def slot_keys(routes, experts, capacity):
    rows = routes.shape[0]
    lanes = lax.broadcasted_iota(jnp.int32, (rows, experts), 1)
    named = [(routes[:, k : k + 1] == lanes).astype(jnp.float32) for k in range(TOP)]
    counts = sum(named).astype(jnp.bfloat16)
    below = lax.broadcasted_iota(jnp.int32, (rows, rows), 0) > lax.broadcasted_iota(jnp.int32, (rows, rows), 1)
    earlier = jnp.dot(below.astype(jnp.bfloat16), counts, preferred_element_type=jnp.float32)
    keys = []
    for k in range(TOP):
        place = jnp.sum(earlier * named[k], axis=1, keepdims=True).astype(jnp.int32)
        keys.append(routes[:, k : k + 1] * capacity + place)
    return keys


def pack_kernel(experts, capacity, x_ref, gain_ref, routes_ref, out_ref, scale_ref, pick_ref):
    tile = out_ref.shape[1]
    step = pl.program_id(0)

    @pl.when(step == 0)
    def _():
        values = x_ref[...].astype(jnp.float32)
        scale_ref[...] = lax.rsqrt(jnp.mean(values * values, axis=-1, keepdims=True) + EPSILON)
        keys = slot_keys(routes_ref[...], experts, capacity)
        slots = lax.broadcasted_iota(jnp.int32, (x_ref.shape[0], experts * capacity), 1)
        taken = (keys[0] == slots) | (keys[1] == slots)
        pick_ref[...] = jnp.where(taken, 1.0, 0.0).astype(jnp.bfloat16)

    columns = pl.ds(pl.multiple_of(step * tile, tile), tile)
    values = x_ref[:, columns].astype(jnp.float32)
    normed = (values * scale_ref[...] * gain_ref[:, columns]).astype(jnp.bfloat16)
    out_ref[...] = lax.dot_general(
        pick_ref[...], normed, (((0,), (0,)), ((), ())), preferred_element_type=jnp.float32
    ).astype(jnp.bfloat16)


def pack(x, gain, routes, experts, capacity, tile=512):
    rows, width = x.shape
    slots = experts * capacity
    return pl.pallas_call(
        functools.partial(pack_kernel, experts, capacity),
        grid=(width // tile,),
        in_specs=[
            pl.BlockSpec((rows, width), lambda i: (0, 0)),
            pl.BlockSpec((1, width), lambda i: (0, 0)),
            pl.BlockSpec((rows, TOP), lambda i: (0, 0)),
        ],
        out_specs=pl.BlockSpec((slots, tile), lambda i: (0, i)),
        out_shape=jax.ShapeDtypeStruct((slots, width), jnp.bfloat16),
        scratch_shapes=[pltpu.VMEM((rows, 1), jnp.float32), pltpu.VMEM((rows, slots), jnp.bfloat16)],
        compiler_params=pltpu.CompilerParams(vmem_limit_bytes=VMEM_LIMIT),
        cost_estimate=pl.CostEstimate(flops=2 * rows * slots * width, bytes_accessed=2 * (rows + slots) * width, transcendentals=0),
        name="pack",
    )(x, gain, routes)


def mlp_kernel(up_tiles, rows_ref, gate_ref, up_ref, down_ref, out_ref, hidden_ref):
    step = pl.program_id(0)
    tile = gate_ref.shape[1]

    @pl.when(step < up_tiles)
    def _():
        rows = rows_ref[...]
        gate = jnp.dot(rows, gate_ref[...], preferred_element_type=jnp.float32)
        upward = jnp.dot(rows, up_ref[...], preferred_element_type=jnp.float32)
        columns = pl.ds(pl.multiple_of(step * tile, tile), tile)
        hidden_ref[:, columns] = (jax.nn.silu(gate) * upward).astype(jnp.bfloat16)

    @pl.when(step >= up_tiles)
    def _():
        out_ref[...] = jnp.dot(
            hidden_ref[...], down_ref[...], preferred_element_type=jnp.float32
        ).astype(jnp.bfloat16)


def mlp(rows, gate_matrix, up_matrix, down_matrix, up_tile=256, down_tile=512):
    slots, width = rows.shape
    inner = gate_matrix.shape[1]
    up_tiles, down_tiles = inner // up_tile, width // down_tile
    return pl.pallas_call(
        functools.partial(mlp_kernel, up_tiles),
        grid=(up_tiles + down_tiles,),
        in_specs=[
            pl.BlockSpec((slots, width), lambda i: (0, 0), pipeline_mode=pl.Buffered(1)),
            pl.BlockSpec((width, up_tile), lambda i: (0, jnp.minimum(i, up_tiles - 1))),
            pl.BlockSpec((width, up_tile), lambda i: (0, jnp.minimum(i, up_tiles - 1))),
            pl.BlockSpec((inner, down_tile), lambda i: (0, jnp.maximum(i - up_tiles, 0))),
        ],
        out_specs=pl.BlockSpec((slots, down_tile), lambda i: (0, jnp.maximum(i - up_tiles, 0))),
        out_shape=jax.ShapeDtypeStruct((slots, width), jnp.bfloat16),
        scratch_shapes=[pltpu.VMEM((slots, inner), jnp.bfloat16)],
        compiler_params=pltpu.CompilerParams(vmem_limit_bytes=VMEM_LIMIT),
        cost_estimate=pl.CostEstimate(
            flops=6 * slots * width * inner,
            bytes_accessed=2 * (2 * slots * width + 3 * width * inner),
            transcendentals=slots * inner,
        ),
        name="mlp",
    )(rows, gate_matrix, up_matrix, down_matrix)


def combine_kernel(experts, capacity, back_ref, x_ref, routes_ref, logits_ref, out_ref, weight_ref):
    rows = x_ref.shape[0]

    @pl.when(pl.program_id(0) == 0)
    def _():
        lifted = jax.nn.sigmoid(logits_ref[...])
        shares = lifted / jnp.sum(lifted, axis=-1, keepdims=True)
        keys = slot_keys(routes_ref[...], experts, capacity)
        slots = lax.broadcasted_iota(jnp.int32, (rows, experts * capacity), 1)
        weight = sum(jnp.where(keys[k] == slots, shares[:, k : k + 1], 0.0) for k in range(TOP))
        coarse = weight.astype(jnp.bfloat16)
        weight_ref[:rows, :] = coarse
        weight_ref[rows:, :] = (weight - coarse.astype(jnp.float32)).astype(jnp.bfloat16)

    mixed = jnp.dot(weight_ref[...], back_ref[...], preferred_element_type=jnp.float32)
    out_ref[...] = (x_ref[...].astype(jnp.float32) + (mixed[:rows] + mixed[rows:])).astype(jnp.bfloat16)


def combine(back, x, routes, logits, experts, capacity, tile=512):
    slots, width = back.shape
    rows = x.shape[0]
    return pl.pallas_call(
        functools.partial(combine_kernel, experts, capacity),
        grid=(width // tile,),
        in_specs=[
            pl.BlockSpec((slots, tile), lambda i: (0, i)),
            pl.BlockSpec((rows, tile), lambda i: (0, i)),
            pl.BlockSpec((rows, TOP), lambda i: (0, 0)),
            pl.BlockSpec((rows, TOP), lambda i: (0, 0)),
        ],
        out_specs=pl.BlockSpec((rows, tile), lambda i: (0, i)),
        out_shape=jax.ShapeDtypeStruct((rows, width), jnp.bfloat16),
        scratch_shapes=[pltpu.VMEM((2 * rows, slots), jnp.bfloat16)],
        compiler_params=pltpu.CompilerParams(vmem_limit_bytes=VMEM_LIMIT),
        cost_estimate=pl.CostEstimate(flops=4 * rows * slots * width, bytes_accessed=2 * (2 * rows + slots) * width, transcendentals=0),
        name="combine",
    )(back, x, routes, logits)


def exchange(blocks, experts, capacity):
    width = blocks.shape[1]
    moved = lax.all_to_all(blocks.reshape(experts, capacity, width), "expert", 0, 0, tiled=True)
    return moved.reshape(experts * capacity, width)


def shifted(value):
    count = lax.axis_size("section")
    return lax.ppermute(value, "section", [(i, (i + 1) % count) for i in range(count)])


def on_device(activations, norm_gain, w_gate, w_up, w_down, routes, gate_logits):
    experts = lax.axis_size("expert")
    capacity = 2 * activations.shape[1] * TOP // experts
    current = activations[0]
    for step in range(STEPS):
        chosen, logits = routes[step, 0], gate_logits[step, 0]
        packed = pack(current, norm_gain, chosen, experts, capacity)
        rows = exchange(packed, experts, capacity)
        produced = mlp(rows, w_gate[0, 0], w_up[0, 0], w_down[0, 0])
        back = exchange(produced, experts, capacity)
        current = shifted(combine(back, current, chosen, logits, experts, capacity))
    return current[None]


def solution(mesh):
    in_specs = (
        P("section", "expert", None),
        P("section", None),
        P("section", "expert", None, None),
        P("section", "expert", None, None),
        P("section", "expert", None, None),
        P(None, "section", "expert", None),
        P(None, "section", "expert", None),
    )
    return jax.shard_map(
        on_device, mesh=mesh, in_specs=in_specs, out_specs=P("section", "expert", None), check_vma=False
    )
```

```python
import functools

import jax
import jax.numpy as jnp
from jax import lax
from jax.experimental import pallas as pl
from jax.experimental.pallas import tpu as pltpu
from jax.sharding import PartitionSpec as P

TOP = 2
STEPS = 2
EPSILON = 1e-06
VMEM_LIMIT = 56 * 1024 * 1024
PARAMS = pltpu.CompilerParams(vmem_limit_bytes=VMEM_LIMIT)
ANY = pl.BlockSpec(memory_space=pl.ANY)
VMEM = pl.BlockSpec(memory_space=pltpu.VMEM)


def slot_rows(routes, experts, capacity):
    rows = routes.shape[1]
    lines = lax.broadcasted_iota(jnp.int32, (experts, rows), 0)
    named = [(routes[k : k + 1] == lines).astype(jnp.float32) for k in range(TOP)]
    counts = sum(named).astype(jnp.bfloat16)
    before = lax.broadcasted_iota(jnp.int32, (rows, rows), 0) < lax.broadcasted_iota(jnp.int32, (rows, rows), 1)
    earlier = jnp.dot(counts, jnp.where(before, 1.0, 0.0).astype(jnp.bfloat16), preferred_element_type=jnp.float32)
    return [
        routes[k : k + 1] * capacity + jnp.sum(earlier * named[k], axis=0, keepdims=True).astype(jnp.int32)
        for k in range(TOP)
    ]


def cuts(total, size):
    return [(start, min(size, total - start)) for start in range(0, total, size)]


def pack_kernel(experts, capacity, tile, x_ref, gain_ref, routes_ref, out_ref, held_ref, sems):
    rows, width = x_ref.shape
    slots = experts * capacity
    keys = slot_rows(routes_ref[...], experts, capacity)
    lines = lax.broadcasted_iota(jnp.int32, (slots, rows), 0)
    pick = jnp.where((keys[0] == lines) | (keys[1] == lines), 1.0, 0.0).astype(jnp.bfloat16)
    values = x_ref[...].astype(jnp.float32)
    scale = lax.rsqrt(jnp.mean(values * values, axis=-1, keepdims=True) + EPSILON)
    copies = []
    for i, (start, size) in enumerate(cuts(width, tile)):
        part = x_ref[:, start : start + size].astype(jnp.float32)
        normed = (part * scale * gain_ref[:, start : start + size]).astype(jnp.bfloat16)
        held_ref[:, start : start + size] = jnp.dot(pick, normed, preferred_element_type=jnp.float32).astype(jnp.bfloat16)
        copy = pltpu.make_async_copy(held_ref.at[:, start : start + size], out_ref.at[:, start : start + size], sems.at[i])
        copy.start()
        copies.append(copy)
    for copy in copies:
        copy.wait()


def pack(x, gain, routes, experts, capacity, tile=512):
    rows, width = x.shape
    slots = experts * capacity
    return pl.pallas_call(
        functools.partial(pack_kernel, experts, capacity, tile),
        in_specs=[VMEM, VMEM, VMEM],
        out_specs=ANY,
        out_shape=jax.ShapeDtypeStruct((slots, width), jnp.bfloat16),
        scratch_shapes=[pltpu.VMEM((slots, width), jnp.bfloat16), pltpu.SemaphoreType.DMA((len(cuts(width, tile)),))],
        compiler_params=PARAMS,
        cost_estimate=pl.CostEstimate(flops=2 * rows * slots * width, bytes_accessed=2 * (rows + slots) * width, transcendentals=0),
        name="pack",
    )(x, gain, routes)


def mlp_kernel(first_cut, in_tile, down_cuts, rows_hbm, gate_hbm, up_hbm, down_hbm, out_hbm,
               rows_ref, in_ref, total_ref, down_ref, hidden_ref, out_ref, row_sems, in_sems, down_sems, out_sems):
    width, inner = gate_hbm.shape
    first = cuts(width, first_cut)
    tiles = inner // in_tile

    def in_copies(tile, start, size, i):
        lines = pl.ds(start, size)
        place = 2 * in_tile * tile
        return [
            pltpu.make_async_copy(
                source.at[lines, pl.ds(tile * in_tile, in_tile)],
                in_ref.at[lines, pl.ds(place + k * in_tile, in_tile)],
                in_sems.at[2 * i + k],
            )
            for k, source in enumerate((gate_hbm, up_hbm))
        ]

    opening = []
    for i, (start, size) in enumerate(first):
        row_copy = pltpu.make_async_copy(rows_hbm.at[:, pl.ds(start, size)], rows_ref.at[:, pl.ds(start, size)], row_sems.at[i])
        opening.append([row_copy, *in_copies(0, start, size, i)])
    later = [in_copies(t, 0, width, len(first) + t - 1) for t in range(1, tiles)]
    later += [
        [pltpu.make_async_copy(down_hbm.at[:, pl.ds(start, size)], down_ref.at[:, pl.ds(start, size)], down_sems.at[i])]
        for i, (start, size) in enumerate(down_cuts)
    ]

    def begin(group):
        for copy in group:
            copy.start()

    def finish(group):
        for copy in group:
            copy.wait()

    for group in opening:
        begin(group)
    ahead = 2
    for group in later[:ahead]:
        begin(group)

    def activate(tile, both):
        gate, upward = both[:, :in_tile], both[:, in_tile:]
        hidden_ref[:, tile * in_tile : (tile + 1) * in_tile] = (jax.nn.silu(gate) * upward).astype(jnp.bfloat16)

    for i, (start, size) in enumerate(first):
        finish(opening[i])
        part = jnp.dot(rows_ref[:, start : start + size], in_ref[start : start + size, : 2 * in_tile], preferred_element_type=jnp.float32)
        if i == 0:
            total_ref[...] = part
        else:
            total_ref[...] += part
    activate(0, total_ref[...])
    for tile in range(1, tiles):
        if tile - 1 + ahead < len(later):
            begin(later[tile - 1 + ahead])
        finish(later[tile - 1])
        place = 2 * in_tile * tile
        activate(tile, jnp.dot(rows_ref[...], in_ref[:, place : place + 2 * in_tile], preferred_element_type=jnp.float32))
    sent = []
    for i, (start, size) in enumerate(down_cuts):
        if tiles - 1 + i + ahead < len(later):
            begin(later[tiles - 1 + i + ahead])
        finish(later[tiles - 1 + i])
        out_ref[:, start : start + size] = jnp.dot(
            hidden_ref[...], down_ref[:, start : start + size], preferred_element_type=jnp.float32
        ).astype(jnp.bfloat16)
        copy = pltpu.make_async_copy(out_ref.at[:, pl.ds(start, size)], out_hbm.at[:, pl.ds(start, size)], out_sems.at[i])
        copy.start()
        sent.append(copy)
    finish(sent)


def mlp(rows, gate_matrix, up_matrix, down_matrix, first_cut=512, in_tile=512, down_tile=1024):
    slots, width = rows.shape
    inner = gate_matrix.shape[1]
    down_cuts = cuts(width, down_tile)
    first, tiles = len(cuts(width, first_cut)), inner // in_tile
    dma = pltpu.SemaphoreType.DMA
    return pl.pallas_call(
        functools.partial(mlp_kernel, first_cut, in_tile, down_cuts),
        in_specs=[ANY] * 4,
        out_specs=ANY,
        out_shape=jax.ShapeDtypeStruct((slots, width), jnp.bfloat16),
        scratch_shapes=[
            pltpu.VMEM((slots, width), jnp.bfloat16),
            pltpu.VMEM((width, 2 * inner), jnp.bfloat16),
            pltpu.VMEM((slots, 2 * in_tile), jnp.float32),
            pltpu.VMEM((inner, width), jnp.bfloat16),
            pltpu.VMEM((slots, inner), jnp.bfloat16),
            pltpu.VMEM((slots, width), jnp.bfloat16),
            dma((first,)),
            dma((2 * (first + tiles - 1),)),
            dma((len(down_cuts),)),
            dma((len(down_cuts),)),
        ],
        compiler_params=PARAMS,
        cost_estimate=pl.CostEstimate(
            flops=6 * slots * width * inner,
            bytes_accessed=2 * (2 * slots * width + 3 * width * inner),
            transcendentals=slots * inner,
        ),
        name="mlp",
    )(rows, gate_matrix, up_matrix, down_matrix)


def combine_kernel(experts, capacity, tile, back_hbm, x_hbm, routes_ref, logits_ref, out_hbm, back_ref, x_ref, out_ref, sems, out_sems):
    rows, width = x_ref.shape
    slots = experts * capacity
    copies = []
    for i, (start, size) in enumerate(cuts(width, tile)):
        copy = pltpu.make_async_copy(back_hbm.at[:, pl.ds(start, size)], back_ref.at[:, pl.ds(start, size)], sems.at[i])
        copy.start()
        copies.append(copy)
        if i == 0:
            x_copy = pltpu.make_async_copy(x_hbm, x_ref, sems.at[len(cuts(width, tile))])
            x_copy.start()
    lifted = jax.nn.sigmoid(logits_ref[...])
    shares = lifted / jnp.sum(lifted, axis=0, keepdims=True)
    keys = slot_rows(routes_ref[...], experts, capacity)
    lines = lax.broadcasted_iota(jnp.int32, (slots, rows), 0)
    weight = sum(jnp.where(keys[k] == lines, shares[k : k + 1], 0.0) for k in range(TOP)).T
    coarse = weight.astype(jnp.bfloat16)
    fine = (weight - coarse.astype(jnp.float32)).astype(jnp.bfloat16)
    both = jnp.concatenate([coarse, fine], axis=0)
    x_copy.wait()
    sent = []
    for i, (start, size) in enumerate(cuts(width, tile)):
        copies[i].wait()
        mixed = jnp.dot(both, back_ref[:, start : start + size], preferred_element_type=jnp.float32)
        out_ref[:, start : start + size] = (
            x_ref[:, start : start + size].astype(jnp.float32) + (mixed[:rows] + mixed[rows:])
        ).astype(jnp.bfloat16)
        copy = pltpu.make_async_copy(out_ref.at[:, pl.ds(start, size)], out_hbm.at[:, pl.ds(start, size)], out_sems.at[i])
        copy.start()
        sent.append(copy)
    for copy in sent:
        copy.wait()


def combine(back, x, routes, logits, experts, capacity, tile=896):
    slots, width = back.shape
    rows = x.shape[0]
    return pl.pallas_call(
        functools.partial(combine_kernel, experts, capacity, tile),
        in_specs=[ANY, ANY, VMEM, VMEM],
        out_specs=ANY,
        out_shape=jax.ShapeDtypeStruct((rows, width), jnp.bfloat16),
        scratch_shapes=[
            pltpu.VMEM((slots, width), jnp.bfloat16),
            pltpu.VMEM((rows, width), jnp.bfloat16),
            pltpu.VMEM((rows, width), jnp.bfloat16),
            pltpu.SemaphoreType.DMA((len(cuts(width, tile)) + 1,)),
            pltpu.SemaphoreType.DMA((len(cuts(width, tile)),)),
        ],
        compiler_params=PARAMS,
        cost_estimate=pl.CostEstimate(flops=4 * rows * slots * width, bytes_accessed=2 * (2 * rows + slots) * width, transcendentals=0),
        name="combine",
    )(back, x, routes, logits)


def exchange(blocks, experts, capacity):
    width = blocks.shape[1]
    moved = lax.all_to_all(blocks.reshape(experts, capacity, width), "expert", 0, 0, tiled=True)
    return moved.reshape(experts * capacity, width)


def moved_from(value, odd):
    count = lax.axis_size("section")
    return lax.ppermute(value, "section", [(i, (i + 1) % count) for i in range(count) if i % 2 == odd])


def on_device(activations, norm_gain, w_gate, w_up, w_down, routes, gate_logits):
    experts = lax.axis_size("expert")
    capacity = 2 * activations.shape[1] * TOP // experts
    chosen = [routes[step, 0].T for step in range(STEPS)]
    logits = [gate_logits[step, 0].T for step in range(STEPS)]

    def layer(step, current):
        packed = pack(current, norm_gain, chosen[step], experts, capacity)
        rows = exchange(packed, experts, capacity)
        produced = mlp(rows, w_gate[0, 0], w_up[0, 0], w_down[0, 0])
        back = exchange(produced, experts, capacity)
        return combine(back, current, chosen[step], logits[step], experts, capacity)

    odd = lax.axis_index("section") % 2 == 1
    first = layer(0, activations[0])
    near, far = moved_from(first, 0), moved_from(first, 1)
    early = lax.cond(odd, lambda: layer(1, near), lambda: jnp.zeros_like(first))
    far_out = moved_from(early, 1)
    late = lax.cond(odd, lambda: jnp.zeros_like(first), lambda: layer(1, far))
    near_out = moved_from(late, 0)
    return jnp.where(odd, near_out, far_out)[None]


def solution(mesh):
    in_specs = (
        P("section", "expert", None),
        P("section", None),
        P("section", "expert", None, None),
        P("section", "expert", None, None),
        P("section", "expert", None, None),
        P(None, "section", "expert", None),
        P(None, "section", "expert", None),
    )
    return jax.shard_map(
        on_device, mesh=mesh, in_specs=in_specs, out_specs=P("section", "expert", None), check_vma=False
    )
```

```python
import functools

import jax
import jax.numpy as jnp
from jax import lax
from jax.experimental import pallas as pl
from jax.experimental.pallas import tpu as pltpu
from jax.sharding import PartitionSpec as P

TOP = 2
STEPS = 2
EPSILON = 1e-06
VMEM_LIMIT = 56 * 1024 * 1024
PARAMS = pltpu.CompilerParams(vmem_limit_bytes=VMEM_LIMIT)
ANY = pl.BlockSpec(memory_space=pl.ANY)
VMEM = pl.BlockSpec(memory_space=pltpu.VMEM)


def slot_rows(routes, experts, capacity):
    rows = routes.shape[1]
    lines = lax.broadcasted_iota(jnp.int32, (experts, rows), 0)
    named = [(routes[k : k + 1] == lines).astype(jnp.float32) for k in range(TOP)]
    counts = sum(named).astype(jnp.bfloat16)
    before = lax.broadcasted_iota(jnp.int32, (rows, rows), 0) < lax.broadcasted_iota(jnp.int32, (rows, rows), 1)
    earlier = jnp.dot(counts, jnp.where(before, 1.0, 0.0).astype(jnp.bfloat16), preferred_element_type=jnp.float32)
    return [
        routes[k : k + 1] * capacity + jnp.sum(earlier * named[k], axis=0, keepdims=True).astype(jnp.int32)
        for k in range(TOP)
    ]


def cuts(total, size):
    return [(start, min(size, total - start)) for start in range(0, total, size)]


def pack_kernel(step, experts, capacity, tile, widths, *refs):
    if widths:
        flag_ref, x_ref, gain_ref, routes_ref, whole_hbm, *parts, held_ref, sems = refs
    else:
        x_ref, gain_ref, routes_ref, whole_hbm, held_ref, sems = refs
        parts = []
    rows, width = x_ref.shape
    slots = experts * capacity
    keys = slot_rows(routes_ref[step], experts, capacity)
    lines = lax.broadcasted_iota(jnp.int32, (slots, rows), 0)
    pick = jnp.where((keys[0] == lines) | (keys[1] == lines), 1.0, 0.0).astype(jnp.bfloat16)
    values = x_ref[...].astype(jnp.float32)
    scale = lax.rsqrt(jnp.mean(values * values, axis=-1, keepdims=True) + EPSILON)
    targets = [part.at[:, start : start + tile] for part, size in zip(parts, widths) for start in range(0, size, tile)]

    def each(i, start, size, act):
        source = held_ref.at[:, start : start + size]
        whole = pltpu.make_async_copy(source, whole_hbm.at[:, start : start + size], sems.at[i])
        if targets:
            part = pltpu.make_async_copy(source, targets[i], sems.at[i])
            pl.when(flag_ref[0] == 0)(lambda: act(whole))
            pl.when(flag_ref[0] == 1)(lambda: act(part))
        else:
            act(whole)

    for i, (start, size) in enumerate(cuts(width, tile)):
        values = x_ref[:, start : start + size].astype(jnp.float32)
        normed = (values * scale * gain_ref[:, start : start + size]).astype(jnp.bfloat16)
        held_ref[:, start : start + size] = jnp.dot(pick, normed, preferred_element_type=jnp.float32).astype(jnp.bfloat16)
        each(i, start, size, lambda copy: copy.start())
    for i, (start, size) in enumerate(cuts(width, tile)):
        each(i, start, size, lambda copy: copy.wait())


def pack(step, x, gain, routes, experts, capacity, flag=None, widths=(), tile=512):
    rows, width = x.shape
    slots = experts * capacity
    shapes = [jax.ShapeDtypeStruct((slots, size), jnp.bfloat16) for size in (width, *widths)]
    flags = [flag] if widths else []
    out = pl.pallas_call(
        functools.partial(pack_kernel, step, experts, capacity, tile, widths),
        in_specs=[pl.BlockSpec(memory_space=pltpu.SMEM)] * len(flags) + [VMEM, VMEM, VMEM],
        out_specs=[ANY] * len(shapes),
        out_shape=shapes,
        scratch_shapes=[pltpu.VMEM((slots, width), jnp.bfloat16), pltpu.SemaphoreType.DMA((len(cuts(width, tile)),))],
        compiler_params=PARAMS,
        cost_estimate=pl.CostEstimate(flops=2 * rows * slots * width, bytes_accessed=2 * (rows + slots) * width, transcendentals=0),
        name="pack",
    )(*flags, x, gain, routes)
    return out if widths else out[0]


def mlp_kernel(widths, turn, depth, in_tile, down_tile, *refs):
    sources = refs[: len(widths)]
    gate_hbm, up_hbm, down_hbm, *_, out_hbm = refs[len(widths) : -11]
    rows_ref, in_ref, total_ref, down_ref, hidden_ref, out_ref, row_sems, first_sems, in_sems, down_sems, out_sems = refs[-11:]
    slots = rows_ref.shape[0]
    width, inner = gate_hbm.shape
    depths, tiles, downs = width // depth, inner // in_tile, width // down_tile

    def span(index, size):
        return pl.ds(pl.multiple_of(index * size, size), size)

    def first_copies(i):
        lines = span(i, depth)
        return [
            pltpu.make_async_copy(
                source.at[lines, pl.ds(0, in_tile)], in_ref.at[lines, pl.ds(k * in_tile, in_tile)], first_sems.at[k, i]
            )
            for k, source in enumerate((gate_hbm, up_hbm))
        ]

    def in_copies(tile):
        return [
            pltpu.make_async_copy(source.at[:, span(tile, in_tile)], in_ref.at[:, span(2 * tile + k, in_tile)], in_sems.at[k, tile])
            for k, source in enumerate((gate_hbm, up_hbm))
        ]

    def down_copies(i):
        return [pltpu.make_async_copy(down_hbm.at[:, span(i, down_tile)], down_ref.at[:, span(i, down_tile)], down_sems.at[i])]

    def out_copies(i):
        pieces = [(0, turn, slots - turn), (slots - turn, 0, turn)] if turn else [(0, 0, slots)]
        return [
            pltpu.make_async_copy(
                out_ref.at[pl.ds(source, lines), span(i, down_tile)],
                out_hbm.at[pl.ds(target, lines), span(i, down_tile)],
                out_sems.at[k, i],
            )
            for k, (source, target, lines) in enumerate(pieces)
        ]

    def begin(copies):
        for copy in copies:
            copy.start()

    def finish(copies):
        for copy in copies:
            copy.wait()

    def activate(tile, both):
        gate, upward = both[:, :in_tile], both[:, in_tile:]
        hidden_ref[:, span(tile, in_tile)] = (jax.nn.silu(gate) * upward).astype(jnp.bfloat16)

    places = [(source, start) for source, size in zip(sources, widths) for start in range(0, size, depth)]
    for i, (source, start) in enumerate(places):
        pltpu.make_async_copy(source.at[:, start : start + depth], rows_ref.at[:, span(i, depth)], row_sems.at[i]).start()
        begin(first_copies(i))
    begin(in_copies(1))

    def opening(i, carry):
        pltpu.make_async_copy(sources[0].at[:, :depth], rows_ref.at[:, span(i, depth)], row_sems.at[i]).wait()
        finish(first_copies(i))
        total_ref[...] = jnp.where(i == 0, 0.0, total_ref[...]) + jnp.dot(
            rows_ref[:, span(i, depth)], in_ref[span(i, depth), pl.ds(0, 2 * in_tile)], preferred_element_type=jnp.float32
        )
        return carry

    lax.fori_loop(0, depths, opening, 0)
    begin(in_copies(2))
    activate(0, total_ref[...])

    def inward(tile, carry):
        @pl.when(tile < tiles - 2)
        def _():
            begin(in_copies(tile + 2))

        @pl.when(tile >= tiles - 2)
        def _():
            begin(down_copies(2 * (tile - tiles + 2)))
            begin(down_copies(2 * (tile - tiles + 2) + 1))

        finish(in_copies(tile))
        activate(tile, jnp.dot(rows_ref[...], in_ref[:, span(tile, 2 * in_tile)], preferred_element_type=jnp.float32))
        return carry

    lax.fori_loop(1, tiles, inward, 0)

    def outward(i, carry):
        finish(down_copies(i))
        out_ref[:, span(i, down_tile)] = jnp.dot(
            hidden_ref[...], down_ref[:, span(i, down_tile)], preferred_element_type=jnp.float32
        ).astype(jnp.bfloat16)
        begin(out_copies(i))
        return carry

    lax.fori_loop(0, downs, outward, 0)
    for i in range(downs):
        finish(out_copies(i))


def mlp(rows, gate_matrix, up_matrix, down_matrix, *after, turn=0, depth=512, in_tile=256, down_tile=896):
    slots, width = rows[0].shape[0], gate_matrix.shape[0]
    widths = [part.shape[1] for part in rows]
    inner = gate_matrix.shape[1]
    depths, tiles, downs = width // depth, inner // in_tile, width // down_tile
    dma = pltpu.SemaphoreType.DMA
    return pl.pallas_call(
        functools.partial(mlp_kernel, widths, turn, depth, in_tile, down_tile),
        in_specs=[ANY] * (len(rows) + 3 + len(after)),
        out_specs=ANY,
        out_shape=jax.ShapeDtypeStruct((slots, width), jnp.bfloat16),
        scratch_shapes=[
            pltpu.VMEM((slots, width), jnp.bfloat16),
            pltpu.VMEM((width, 2 * inner), jnp.bfloat16),
            pltpu.VMEM((slots, 2 * in_tile), jnp.float32),
            pltpu.VMEM((inner, width), jnp.bfloat16),
            pltpu.VMEM((slots, inner), jnp.bfloat16),
            pltpu.VMEM((slots, width), jnp.bfloat16),
            dma((depths,)),
            dma((2, depths)),
            dma((2, tiles)),
            dma((downs,)),
            dma((2, downs)),
        ],
        compiler_params=PARAMS,
        cost_estimate=pl.CostEstimate(
            flops=6 * slots * width * inner,
            bytes_accessed=2 * (2 * slots * width + 3 * width * inner),
            transcendentals=slots * inner,
        ),
        name="mlp",
    )(*rows, gate_matrix, up_matrix, down_matrix, *after)


def combine_kernel(step, experts, capacity, tile, back_hbm, x_hbm, routes_ref, logits_ref, out_hbm, back_ref, x_ref, out_ref, sems, out_sems):
    rows, width = x_ref.shape
    slots = experts * capacity
    copies = []
    for i, (start, size) in enumerate(cuts(width, tile)):
        copy = pltpu.make_async_copy(back_hbm.at[:, pl.ds(start, size)], back_ref.at[:, pl.ds(start, size)], sems.at[i])
        copy.start()
        copies.append(copy)
        if i == 0:
            x_copy = pltpu.make_async_copy(x_hbm, x_ref, sems.at[len(cuts(width, tile))])
            x_copy.start()
    lifted = jax.nn.sigmoid(logits_ref[step])
    shares = lifted / jnp.sum(lifted, axis=0, keepdims=True)
    keys = slot_rows(routes_ref[step], experts, capacity)
    lines = lax.broadcasted_iota(jnp.int32, (slots, rows), 0)
    weight = sum(jnp.where(keys[k] == lines, shares[k : k + 1], 0.0) for k in range(TOP)).T
    coarse = weight.astype(jnp.bfloat16)
    fine = (weight - coarse.astype(jnp.float32)).astype(jnp.bfloat16)
    both = jnp.concatenate([coarse, fine], axis=0)
    x_copy.wait()
    sent = []
    for i, (start, size) in enumerate(cuts(width, tile)):
        copies[i].wait()
        mixed = jnp.dot(both, back_ref[:, start : start + size], preferred_element_type=jnp.float32)
        out_ref[:, start : start + size] = (
            x_ref[:, start : start + size].astype(jnp.float32) + (mixed[:rows] + mixed[rows:])
        ).astype(jnp.bfloat16)
        copy = pltpu.make_async_copy(out_ref.at[:, pl.ds(start, size)], out_hbm.at[:, pl.ds(start, size)], out_sems.at[i])
        copy.start()
        sent.append(copy)
    for copy in sent:
        copy.wait()


def combine(step, back, x, routes, logits, experts, capacity, tile=896):
    slots, width = back.shape
    rows = x.shape[0]
    return pl.pallas_call(
        functools.partial(combine_kernel, step, experts, capacity, tile),
        in_specs=[ANY, ANY, VMEM, VMEM],
        out_specs=ANY,
        out_shape=jax.ShapeDtypeStruct((rows, width), jnp.bfloat16),
        scratch_shapes=[
            pltpu.VMEM((slots, width), jnp.bfloat16),
            pltpu.VMEM((rows, width), jnp.bfloat16),
            pltpu.VMEM((rows, width), jnp.bfloat16),
            pltpu.SemaphoreType.DMA((len(cuts(width, tile)) + 1,)),
            pltpu.SemaphoreType.DMA((len(cuts(width, tile)),)),
        ],
        compiler_params=PARAMS,
        cost_estimate=pl.CostEstimate(flops=4 * rows * slots * width, bytes_accessed=2 * (2 * rows + slots) * width, transcendentals=0),
        name="combine",
    )(back, x, routes, logits)
PARTS = (512, 3072)


def exchange(blocks, experts, capacity):
    width = blocks.shape[1]
    moved = lax.all_to_all(blocks.reshape(experts, capacity, width), "expert", 0, 0, tiled=True)
    return moved.reshape(experts * capacity, width)


def moved_from(value, odd, turn=0):
    sections, experts = lax.axis_size("section"), lax.axis_size("expert")
    pairs = [
        (i * experts + j, (i + 1) % sections * experts + (j + turn) % experts)
        for i in range(odd, sections, 2)
        for j in range(experts)
    ]
    return lax.ppermute(value, ("section", "expert"), pairs)


def on_device(activations, norm_gain, w_gate, w_up, w_down, routes, gate_logits):
    experts = lax.axis_size("expert")
    capacity = 2 * activations.shape[1] * TOP // experts
    chosen, logits = (value[:, 0].transpose(0, 2, 1) for value in (routes, gate_logits))
    start = activations[0]
    parity = lax.axis_index("section") % 2
    odd = parity == 1
    nothing = functools.partial(jnp.zeros_like, start)

    def spread(step, current):
        return exchange(pack(step, current, norm_gain, chosen, experts, capacity), experts, capacity)

    def gather(step, current, rows, *after):
        produced = mlp(rows, w_gate[0, 0], w_up[0, 0], w_down[0, 0], *after)
        back = exchange(produced, experts, capacity)
        return combine(step, back, current, chosen, logits, experts, capacity)

    flag = parity.astype(jnp.int32).reshape(1)
    whole, *parts = pack(0, start, norm_gain, chosen, experts, capacity, flag, PARTS)

    def in_turn():
        rows = []
        for part in parts:
            if rows:
                part, rows[-1] = lax.optimization_barrier((part, rows[-1]))
            rows.append(exchange(part, experts, capacity))
        return rows

    first_even = lax.cond(odd, nothing, lambda: gather(0, start, (exchange(whole, experts, capacity),)))
    near = moved_from(first_even, 0)
    first_odd = lax.cond(odd, lambda: gather(0, start, in_turn(), first_even), nothing)
    far = moved_from(first_odd, 1)
    early = lax.cond(odd, lambda: gather(1, near, (spread(1, near),)), nothing)
    far_out = moved_from(early, 1)
    late = lax.cond(odd, nothing, lambda: gather(1, far, (spread(1, far),), early))
    near_out = moved_from(late, 0)
    kept = lax.cond(odd, nothing, lambda: far_out + jnp.bfloat16(0))
    return jnp.where(parity == 0, kept, near_out)[None]


def solution(mesh):
    in_specs = (
        P("section", "expert", None),
        P("section", None),
        P("section", "expert", None, None),
        P("section", "expert", None, None),
        P("section", "expert", None, None),
        P(None, "section", "expert", None),
        P(None, "section", "expert", None),
    )
    return jax.shard_map(
        on_device, mesh=mesh, in_specs=in_specs, out_specs=P("section", "expert", None), check_vma=False
    )
```

```python
import functools

import jax
import jax.numpy as jnp
from jax import lax
from jax.experimental import pallas as pl
from jax.experimental.pallas import tpu as pltpu
from jax.sharding import PartitionSpec as P

TOP = 2
STEPS = 2
EPSILON = 1e-06
MIB = 1024 * 1024
PARAMS = pltpu.CompilerParams(vmem_limit_bytes=16 * MIB)
MLP_PARAMS = pltpu.CompilerParams(vmem_limit_bytes=36 * MIB)
ANY = pl.BlockSpec(memory_space=pl.ANY)
VMEM = pl.BlockSpec(memory_space=pltpu.VMEM)


def slot_rows(routes, experts, capacity):
    rows = routes.shape[1]
    lines = lax.broadcasted_iota(jnp.int32, (experts, rows), 0)
    named = [(routes[k : k + 1] == lines).astype(jnp.float32) for k in range(TOP)]
    counts = sum(named).astype(jnp.bfloat16)
    before = lax.broadcasted_iota(jnp.int32, (rows, rows), 0) < lax.broadcasted_iota(jnp.int32, (rows, rows), 1)
    earlier = jnp.dot(counts, jnp.where(before, 1.0, 0.0).astype(jnp.bfloat16), preferred_element_type=jnp.float32)
    return [
        routes[k : k + 1] * capacity + jnp.sum(earlier * named[k], axis=0, keepdims=True).astype(jnp.int32)
        for k in range(TOP)
    ]


def cuts(total, size):
    return [(start, min(size, total - start)) for start in range(0, total, size)]


def pack_kernel(step, experts, capacity, tile, kinds, *refs):
    if len(kinds) > 1:
        flag_ref, *refs = refs
    x_ref, gain_ref, routes_ref, *outs, held_ref, sems = refs
    rows, width = x_ref.shape
    slots = experts * capacity
    keys = slot_rows(routes_ref[step], experts, capacity)
    lines = lax.broadcasted_iota(jnp.int32, (slots, rows), 0)
    pick = jnp.where((keys[0] == lines) | (keys[1] == lines), 1.0, 0.0).astype(jnp.bfloat16)
    values = x_ref[...].astype(jnp.float32)
    scale = lax.rsqrt(jnp.mean(values * values, axis=-1, keepdims=True) + EPSILON)
    targets = []
    for widths in kinds:
        parts, outs = outs[: len(widths)], outs[len(widths) :]
        targets.append([part.at[:, start : start + tile] for part, size in zip(parts, widths) for start in range(0, size, tile)])

    def each(i, start, size, act):
        copies = [pltpu.make_async_copy(held_ref.at[:, start : start + size], places[i], sems.at[i]) for places in targets]
        if len(copies) == 1:
            act(copies[0])
        else:
            for value, copy in enumerate(copies):
                pl.when(flag_ref[0] == value)(functools.partial(act, copy))

    for i, (start, size) in enumerate(cuts(width, tile)):
        values = x_ref[:, start : start + size].astype(jnp.float32)
        normed = (values * scale * gain_ref[:, start : start + size]).astype(jnp.bfloat16)
        held_ref[:, start : start + size] = jnp.dot(pick, normed, preferred_element_type=jnp.float32).astype(jnp.bfloat16)
        each(i, start, size, lambda copy: copy.start())
    for i, (start, size) in enumerate(cuts(width, tile)):
        each(i, start, size, lambda copy: copy.wait())


def pack(step, x, gain, routes, experts, capacity, *kinds, flag=None, tile=512):
    rows, width = x.shape
    slots = experts * capacity
    shapes = [jax.ShapeDtypeStruct((slots, size), jnp.bfloat16) for widths in kinds for size in widths]
    flags = [flag] if len(kinds) > 1 else []
    return pl.pallas_call(
        functools.partial(pack_kernel, step, experts, capacity, tile, kinds),
        in_specs=[pl.BlockSpec(memory_space=pltpu.SMEM)] * len(flags) + [VMEM, VMEM, VMEM],
        out_specs=[ANY] * len(shapes),
        out_shape=shapes,
        scratch_shapes=[pltpu.VMEM((slots, width), jnp.bfloat16), pltpu.SemaphoreType.DMA((len(cuts(width, tile)),))],
        compiler_params=PARAMS,
        cost_estimate=pl.CostEstimate(flops=2 * rows * slots * width, bytes_accessed=2 * (rows + slots) * width, transcendentals=0),
        name="pack",
    )(*flags, x, gain, routes)


def mlp_kernel(widths, turn, depth, in_tile, down_tile, *refs):
    sources = refs[: len(widths)]
    gate_hbm, up_hbm, down_hbm, *_, out_hbm = refs[len(widths) : -11]
    rows_ref, in_ref, total_ref, down_ref, hidden_ref, out_ref, row_sems, first_sems, in_sems, down_sems, out_sems = refs[-11:]
    slots = rows_ref.shape[0]
    width, inner = gate_hbm.shape
    depths, tiles, downs = width // depth, inner // in_tile, width // down_tile

    def span(index, size):
        return pl.ds(pl.multiple_of(index * size, size), size)

    def first_copies(i):
        lines = span(i, depth)
        return [
            pltpu.make_async_copy(
                source.at[lines, pl.ds(0, in_tile)], in_ref.at[lines, pl.ds(k * in_tile, in_tile)], first_sems.at[k, i]
            )
            for k, source in enumerate((gate_hbm, up_hbm))
        ]

    def in_copies(tile):
        return [
            pltpu.make_async_copy(source.at[:, span(tile, in_tile)], in_ref.at[:, span(2 * tile + k, in_tile)], in_sems.at[k, tile])
            for k, source in enumerate((gate_hbm, up_hbm))
        ]

    def down_copies(i):
        return [pltpu.make_async_copy(down_hbm.at[:, span(i, down_tile)], down_ref.at[:, span(i, down_tile)], down_sems.at[i])]

    def out_copies(i):
        pieces = [(0, turn, slots - turn), (slots - turn, 0, turn)] if turn else [(0, 0, slots)]
        return [
            pltpu.make_async_copy(
                out_ref.at[pl.ds(source, lines), span(i, down_tile)],
                out_hbm.at[pl.ds(target, lines), span(i, down_tile)],
                out_sems.at[k, i],
            )
            for k, (source, target, lines) in enumerate(pieces)
        ]

    def begin(copies):
        for copy in copies:
            copy.start()

    def finish(copies):
        for copy in copies:
            copy.wait()

    def activate(tile, both):
        gate, upward = both[:, :in_tile], both[:, in_tile:]
        hidden_ref[:, span(tile, in_tile)] = (jax.nn.silu(gate) * upward).astype(jnp.bfloat16)

    places = [(source, start) for source, size in zip(sources, widths) for start in range(0, size, depth)]
    for i, (source, start) in enumerate(places):
        pltpu.make_async_copy(source.at[:, start : start + depth], rows_ref.at[:, span(i, depth)], row_sems.at[i]).start()
        begin(first_copies(i))
    begin(in_copies(1))

    def opening(i, carry):
        pltpu.make_async_copy(sources[0].at[:, :depth], rows_ref.at[:, span(i, depth)], row_sems.at[i]).wait()
        finish(first_copies(i))
        total_ref[...] = jnp.where(i == 0, 0.0, total_ref[...]) + jnp.dot(
            rows_ref[:, span(i, depth)], in_ref[span(i, depth), pl.ds(0, 2 * in_tile)], preferred_element_type=jnp.float32
        )
        return carry

    lax.fori_loop(0, depths, opening, 0)
    begin(in_copies(2))
    activate(0, total_ref[...])

    def inward(tile, carry):
        @pl.when(tile < tiles - 2)
        def _():
            begin(in_copies(tile + 2))

        @pl.when(tile >= tiles - 2)
        def _():
            begin(down_copies(2 * (tile - tiles + 2)))
            begin(down_copies(2 * (tile - tiles + 2) + 1))

        finish(in_copies(tile))
        activate(tile, jnp.dot(rows_ref[...], in_ref[:, span(tile, 2 * in_tile)], preferred_element_type=jnp.float32))
        return carry

    lax.fori_loop(1, tiles, inward, 0)

    def outward(i, carry):
        finish(down_copies(i))
        out_ref[:, span(i, down_tile)] = jnp.dot(
            hidden_ref[...], down_ref[:, span(i, down_tile)], preferred_element_type=jnp.float32
        ).astype(jnp.bfloat16)
        begin(out_copies(i))
        return carry

    lax.fori_loop(0, downs, outward, 0)
    for i in range(downs):
        finish(out_copies(i))


def mlp(rows, gate_matrix, up_matrix, down_matrix, *after, turn=0, depth=512, in_tile=256, down_tile=896):
    slots, width = rows[0].shape[0], gate_matrix.shape[0]
    widths = [part.shape[1] for part in rows]
    inner = gate_matrix.shape[1]
    depths, tiles, downs = width // depth, inner // in_tile, width // down_tile
    dma = pltpu.SemaphoreType.DMA
    return pl.pallas_call(
        functools.partial(mlp_kernel, widths, turn, depth, in_tile, down_tile),
        in_specs=[ANY] * (len(rows) + 3 + len(after)),
        out_specs=ANY,
        out_shape=jax.ShapeDtypeStruct((slots, width), jnp.bfloat16),
        scratch_shapes=[
            pltpu.VMEM((slots, width), jnp.bfloat16),
            pltpu.VMEM((width, 2 * inner), jnp.bfloat16),
            pltpu.VMEM((slots, 2 * in_tile), jnp.float32),
            pltpu.VMEM((inner, width), jnp.bfloat16),
            pltpu.VMEM((slots, inner), jnp.bfloat16),
            pltpu.VMEM((slots, width), jnp.bfloat16),
            dma((depths,)),
            dma((2, depths)),
            dma((2, tiles)),
            dma((downs,)),
            dma((2, downs)),
        ],
        compiler_params=MLP_PARAMS,
        cost_estimate=pl.CostEstimate(
            flops=6 * slots * width * inner,
            bytes_accessed=2 * (2 * slots * width + 3 * width * inner),
            transcendentals=slots * inner,
        ),
        name="mlp",
    )(*rows, gate_matrix, up_matrix, down_matrix, *after)


def combine_kernel(step, experts, capacity, tile, back_hbm, x_hbm, routes_ref, logits_ref, out_hbm, back_ref, x_ref, out_ref, sems, out_sems):
    rows, width = x_ref.shape
    slots = experts * capacity
    copies = []
    for i, (start, size) in enumerate(cuts(width, tile)):
        copy = pltpu.make_async_copy(back_hbm.at[:, pl.ds(start, size)], back_ref.at[:, pl.ds(start, size)], sems.at[i])
        copy.start()
        copies.append(copy)
        if i == 0:
            x_copy = pltpu.make_async_copy(x_hbm, x_ref, sems.at[len(cuts(width, tile))])
            x_copy.start()
    lifted = jax.nn.sigmoid(logits_ref[step])
    shares = lifted / jnp.sum(lifted, axis=0, keepdims=True)
    keys = slot_rows(routes_ref[step], experts, capacity)
    lines = lax.broadcasted_iota(jnp.int32, (slots, rows), 0)
    weight = sum(jnp.where(keys[k] == lines, shares[k : k + 1], 0.0) for k in range(TOP)).T
    coarse = weight.astype(jnp.bfloat16)
    fine = (weight - coarse.astype(jnp.float32)).astype(jnp.bfloat16)
    both = jnp.concatenate([coarse, fine], axis=0)
    x_copy.wait()
    sent = []
    for i, (start, size) in enumerate(cuts(width, tile)):
        copies[i].wait()
        mixed = jnp.dot(both, back_ref[:, start : start + size], preferred_element_type=jnp.float32)
        out_ref[:, start : start + size] = (
            x_ref[:, start : start + size].astype(jnp.float32) + (mixed[:rows] + mixed[rows:])
        ).astype(jnp.bfloat16)
        copy = pltpu.make_async_copy(out_ref.at[:, pl.ds(start, size)], out_hbm.at[:, pl.ds(start, size)], out_sems.at[i])
        copy.start()
        sent.append(copy)
    for copy in sent:
        copy.wait()


def combine(step, back, x, routes, logits, experts, capacity, tile=1024):
    slots, width = back.shape
    rows = x.shape[0]
    return pl.pallas_call(
        functools.partial(combine_kernel, step, experts, capacity, tile),
        in_specs=[ANY, ANY, VMEM, VMEM],
        out_specs=ANY,
        out_shape=jax.ShapeDtypeStruct((rows, width), jnp.bfloat16),
        scratch_shapes=[
            pltpu.VMEM((slots, width), jnp.bfloat16),
            pltpu.VMEM((rows, width), jnp.bfloat16),
            pltpu.VMEM((rows, width), jnp.bfloat16),
            pltpu.SemaphoreType.DMA((len(cuts(width, tile)) + 1,)),
            pltpu.SemaphoreType.DMA((len(cuts(width, tile)),)),
        ],
        compiler_params=PARAMS,
        cost_estimate=pl.CostEstimate(flops=4 * rows * slots * width, bytes_accessed=2 * (2 * rows + slots) * width, transcendentals=0),
        name="combine",
    )(back, x, routes, logits)
FIRST_PARTS = (512, 3072)
LAST_PARTS = (3584,)


def exchange(blocks, experts, capacity):
    width = blocks.shape[1]
    moved = lax.all_to_all(blocks.reshape(experts, capacity, width), "expert", 0, 0, tiled=True)
    return moved.reshape(experts * capacity, width)


def moved_from(value, odd):
    sections = lax.axis_size("section")
    return lax.ppermute(value, "section", [(i, (i + 1) % sections) for i in range(odd, sections, 2)])


def on_device(activations, norm_gain, w_gate, w_up, w_down, routes, gate_logits):
    experts = lax.axis_size("expert")
    start = activations[0]
    capacity = 2 * start.shape[0] * TOP // experts
    chosen, logits = (value[:, 0].transpose(0, 2, 1) for value in (routes, gate_logits))
    parity = lax.axis_index("section") % 2
    odd = parity == 1
    nothing = functools.partial(jnp.zeros_like, start)
    whole = (start.shape[1],)

    def in_turn(parts):
        rows = []
        for part in parts:
            if rows:
                part, rows[-1] = lax.optimization_barrier((part, rows[-1]))
            rows.append(exchange(part, experts, capacity))
        return rows

    def layer(step, current, packed, *after):
        produced = mlp(in_turn(packed), w_gate[0, 0], w_up[0, 0], w_down[0, 0], *after)
        back = exchange(produced, experts, capacity)
        return combine(step, back, current, chosen, logits, experts, capacity)

    def packed_rows(step, current, *kinds, flag=None):
        return pack(step, current, norm_gain, chosen, experts, capacity, *kinds, flag=flag)

    flag = parity.astype(jnp.int32).reshape(1)
    packed = packed_rows(0, start, whole, FIRST_PARTS, flag=flag)
    first_even = lax.cond(odd, nothing, lambda: layer(0, start, packed[:1]))
    near = moved_from(first_even, 0)
    first_odd = lax.cond(odd, lambda: layer(0, start, packed[1:], first_even), nothing)
    far = moved_from(first_odd, 1)
    early = lax.cond(odd, lambda: layer(1, near, packed_rows(1, near, whole)), nothing)
    far_out = moved_from(early, 1)
    late = lax.cond(odd, nothing, lambda: layer(1, far, packed_rows(1, far, LAST_PARTS), early))
    near_out = moved_from(late, 0)
    kept = lax.cond(odd, nothing, lambda: far_out + jnp.bfloat16(0))
    return jnp.where(parity == 0, kept, near_out)[None]


def solution(mesh):
    in_specs = (
        P("section", "expert", None),
        P("section", None),
        P("section", "expert", None, None),
        P("section", "expert", None, None),
        P("section", "expert", None, None),
        P(None, "section", "expert", None),
        P(None, "section", "expert", None),
    )
    return jax.shard_map(
        on_device, mesh=mesh, in_specs=in_specs, out_specs=P("section", "expert", None), check_vma=False
    )
```

```python
import functools

import jax
import jax.numpy as jnp
from jax import lax
from jax.experimental import pallas as pl
from jax.experimental.pallas import tpu as pltpu
from jax.sharding import PartitionSpec as P

TOP = 2
STEPS = 2
EPSILON = 1e-06
MIB = 1024 * 1024
PARAMS = pltpu.CompilerParams(vmem_limit_bytes=16 * MIB)
MLP_PARAMS = pltpu.CompilerParams(vmem_limit_bytes=36 * MIB)
ANY = pl.BlockSpec(memory_space=pl.ANY)
VMEM = pl.BlockSpec(memory_space=pltpu.VMEM)


def slot_rows(routes, experts, capacity):
    rows = routes.shape[1]
    lines = lax.broadcasted_iota(jnp.int32, (experts, rows), 0)
    named = [(routes[k : k + 1] == lines).astype(jnp.float32) for k in range(TOP)]
    counts = sum(named).astype(jnp.bfloat16)
    before = lax.broadcasted_iota(jnp.int32, (rows, rows), 0) < lax.broadcasted_iota(jnp.int32, (rows, rows), 1)
    earlier = jnp.dot(counts, jnp.where(before, 1.0, 0.0).astype(jnp.bfloat16), preferred_element_type=jnp.float32)
    return [
        routes[k : k + 1] * capacity + jnp.sum(earlier * named[k], axis=0, keepdims=True).astype(jnp.int32)
        for k in range(TOP)
    ]


def cuts(total, size):
    return [(start, min(size, total - start)) for start in range(0, total, size)]


def pack_kernel(step, experts, capacity, tile, kinds, *refs):
    if len(kinds) > 1:
        flag_ref, *refs = refs
    x_ref, gain_ref, routes_ref, *outs, held_ref, sems = refs
    rows, width = x_ref.shape
    slots = experts * capacity
    keys = slot_rows(routes_ref[step], experts, capacity)
    lines = lax.broadcasted_iota(jnp.int32, (slots, rows), 0)
    pick = jnp.where((keys[0] == lines) | (keys[1] == lines), 1.0, 0.0).astype(jnp.bfloat16)
    values = x_ref[...].astype(jnp.float32)
    scale = lax.rsqrt(jnp.mean(values * values, axis=-1, keepdims=True) + EPSILON)
    targets = []
    for widths in kinds:
        parts, outs = outs[: len(widths)], outs[len(widths) :]
        targets.append([part.at[:, start : start + tile] for part, size in zip(parts, widths) for start in range(0, size, tile)])

    def each(i, start, size, act):
        copies = [pltpu.make_async_copy(held_ref.at[:, start : start + size], places[i], sems.at[i]) for places in targets]
        if len(copies) == 1:
            act(copies[0])
        else:
            for value, copy in enumerate(copies):
                pl.when(flag_ref[0] == value)(functools.partial(act, copy))

    for i, (start, size) in enumerate(cuts(width, tile)):
        values = x_ref[:, start : start + size].astype(jnp.float32)
        normed = (values * scale * gain_ref[:, start : start + size]).astype(jnp.bfloat16)
        held_ref[:, start : start + size] = jnp.dot(pick, normed, preferred_element_type=jnp.float32).astype(jnp.bfloat16)
        each(i, start, size, lambda copy: copy.start())
    for i, (start, size) in enumerate(cuts(width, tile)):
        each(i, start, size, lambda copy: copy.wait())


def pack(step, x, gain, routes, experts, capacity, *kinds, flag=None, tile=896):
    rows, width = x.shape
    slots = experts * capacity
    shapes = [jax.ShapeDtypeStruct((slots, size), jnp.bfloat16) for widths in kinds for size in widths]
    flags = [flag] if len(kinds) > 1 else []
    return pl.pallas_call(
        functools.partial(pack_kernel, step, experts, capacity, tile, kinds),
        in_specs=[pl.BlockSpec(memory_space=pltpu.SMEM)] * len(flags) + [VMEM, VMEM, VMEM],
        out_specs=[ANY] * len(shapes),
        out_shape=shapes,
        scratch_shapes=[pltpu.VMEM((slots, width), jnp.bfloat16), pltpu.SemaphoreType.DMA((len(cuts(width, tile)),))],
        compiler_params=PARAMS,
        cost_estimate=pl.CostEstimate(flops=2 * rows * slots * width, bytes_accessed=2 * (rows + slots) * width, transcendentals=0),
        name="pack",
    )(*flags, x, gain, routes)


def mlp_kernel(widths, turn, depth, in_tile, down_tile, *refs):
    sources = refs[: len(widths)]
    gate_hbm, up_hbm, down_hbm, *_, out_hbm = refs[len(widths) : -11]
    rows_ref, in_ref, total_ref, down_ref, hidden_ref, out_ref, row_sems, first_sems, in_sems, down_sems, out_sems = refs[-11:]
    slots = rows_ref.shape[0]
    width, inner = gate_hbm.shape
    depths, tiles, downs = width // depth, inner // in_tile, width // down_tile

    def span(index, size):
        return pl.ds(index * size if isinstance(index, int) else pl.multiple_of(index * size, size), size)

    def first_copies(i):
        lines = span(i, depth)
        return [
            pltpu.make_async_copy(
                source.at[lines, pl.ds(0, in_tile)], in_ref.at[lines, pl.ds(k * in_tile, in_tile)], first_sems.at[k, i]
            )
            for k, source in enumerate((gate_hbm, up_hbm))
        ]

    def in_copies(tile):
        return [
            pltpu.make_async_copy(source.at[:, span(tile, in_tile)], in_ref.at[:, span(2 * tile + k, in_tile)], in_sems.at[k, tile])
            for k, source in enumerate((gate_hbm, up_hbm))
        ]

    def down_copies(i):
        return [pltpu.make_async_copy(down_hbm.at[:, span(i, down_tile)], down_ref.at[:, span(i, down_tile)], down_sems.at[i])]

    def out_copies(i):
        pieces = [(0, turn, slots - turn), (slots - turn, 0, turn)] if turn else [(0, 0, slots)]
        return [
            pltpu.make_async_copy(
                out_ref.at[pl.ds(source, lines), span(i, down_tile)],
                out_hbm.at[pl.ds(target, lines), span(i, down_tile)],
                out_sems.at[k, i],
            )
            for k, (source, target, lines) in enumerate(pieces)
        ]

    def begin(copies):
        for copy in copies:
            copy.start()

    def finish(copies):
        for copy in copies:
            copy.wait()

    def activate(tile, both):
        gate, upward = both[:, :in_tile], both[:, in_tile:]
        hidden_ref[:, span(tile, in_tile)] = (jax.nn.silu(gate) * upward).astype(jnp.bfloat16)

    places = [(source, start) for source, size in zip(sources, widths) for start in range(0, size, depth)]
    for i, (source, start) in enumerate(places):
        pltpu.make_async_copy(source.at[:, start : start + depth], rows_ref.at[:, span(i, depth)], row_sems.at[i]).start()
        begin(first_copies(i))
    begin(in_copies(1))

    def opening(i, carry):
        pltpu.make_async_copy(sources[0].at[:, :depth], rows_ref.at[:, span(i, depth)], row_sems.at[i]).wait()
        finish(first_copies(i))
        total_ref[...] = jnp.where(i == 0, 0.0, total_ref[...]) + jnp.dot(
            rows_ref[:, span(i, depth)], in_ref[span(i, depth), pl.ds(0, 2 * in_tile)], preferred_element_type=jnp.float32
        )
        return carry

    lax.fori_loop(0, depths, opening, 0, unroll=True)
    begin(in_copies(2))
    activate(0, total_ref[...])

    def inward(tile, carry):
        @pl.when(tile < tiles - 2)
        def _():
            begin(in_copies(tile + 2))

        @pl.when(tile >= tiles - 2)
        def _():
            begin(down_copies(2 * (tile - tiles + 2)))
            begin(down_copies(2 * (tile - tiles + 2) + 1))

        finish(in_copies(tile))
        activate(tile, jnp.dot(rows_ref[...], in_ref[:, span(tile, 2 * in_tile)], preferred_element_type=jnp.float32))
        return carry

    lax.fori_loop(1, tiles, inward, 0)

    def outward(i, carry):
        finish(down_copies(i))
        out_ref[:, span(i, down_tile)] = jnp.dot(
            hidden_ref[...], down_ref[:, span(i, down_tile)], preferred_element_type=jnp.float32
        ).astype(jnp.bfloat16)
        begin(out_copies(i))
        return carry

    for i in range(downs):
        outward(i, 0)
    for i in range(downs):
        finish(out_copies(i))


def mlp(rows, gate_matrix, up_matrix, down_matrix, *after, turn=0, depth=896, in_tile=256, down_tile=896):
    slots, width = rows[0].shape[0], gate_matrix.shape[0]
    widths = [part.shape[1] for part in rows]
    inner = gate_matrix.shape[1]
    depths, tiles, downs = width // depth, inner // in_tile, width // down_tile
    dma = pltpu.SemaphoreType.DMA
    return pl.pallas_call(
        functools.partial(mlp_kernel, widths, turn, depth, in_tile, down_tile),
        in_specs=[ANY] * (len(rows) + 3 + len(after)),
        out_specs=ANY,
        out_shape=jax.ShapeDtypeStruct((slots, width), jnp.bfloat16),
        scratch_shapes=[
            pltpu.VMEM((slots, width), jnp.bfloat16),
            pltpu.VMEM((width, 2 * inner), jnp.bfloat16),
            pltpu.VMEM((slots, 2 * in_tile), jnp.float32),
            pltpu.VMEM((inner, width), jnp.bfloat16),
            pltpu.VMEM((slots, inner), jnp.bfloat16),
            pltpu.VMEM((slots, width), jnp.bfloat16),
            dma((depths,)),
            dma((2, depths)),
            dma((2, tiles)),
            dma((downs,)),
            dma((2, downs)),
        ],
        compiler_params=MLP_PARAMS,
        cost_estimate=pl.CostEstimate(
            flops=6 * slots * width * inner,
            bytes_accessed=2 * (2 * slots * width + 3 * width * inner),
            transcendentals=slots * inner,
        ),
        name="mlp",
    )(*rows, gate_matrix, up_matrix, down_matrix, *after)


def combine_kernel(step, experts, capacity, tile, back_hbm, x_hbm, routes_ref, logits_ref, out_hbm, back_ref, x_ref, out_ref, sems, out_sems):
    rows, width = x_ref.shape
    slots = experts * capacity
    copies = []
    for i, (start, size) in enumerate(cuts(width, tile)):
        copy = pltpu.make_async_copy(back_hbm.at[:, pl.ds(start, size)], back_ref.at[:, pl.ds(start, size)], sems.at[i])
        copy.start()
        copies.append(copy)
        if i == 0:
            x_copy = pltpu.make_async_copy(x_hbm, x_ref, sems.at[len(cuts(width, tile))])
            x_copy.start()
    lifted = jax.nn.sigmoid(logits_ref[step])
    shares = lifted / jnp.sum(lifted, axis=0, keepdims=True)
    keys = slot_rows(routes_ref[step], experts, capacity)
    lines = lax.broadcasted_iota(jnp.int32, (slots, rows), 0)
    weight = sum(jnp.where(keys[k] == lines, shares[k : k + 1], 0.0) for k in range(TOP)).T
    coarse = weight.astype(jnp.bfloat16)
    fine = (weight - coarse.astype(jnp.float32)).astype(jnp.bfloat16)
    both = jnp.concatenate([coarse, fine], axis=0)
    x_copy.wait()
    sent = []
    for i, (start, size) in enumerate(cuts(width, tile)):
        copies[i].wait()
        mixed = jnp.dot(both, back_ref[:, start : start + size], preferred_element_type=jnp.float32)
        out_ref[:, start : start + size] = (
            x_ref[:, start : start + size].astype(jnp.float32) + (mixed[:rows] + mixed[rows:])
        ).astype(jnp.bfloat16)
        copy = pltpu.make_async_copy(out_ref.at[:, pl.ds(start, size)], out_hbm.at[:, pl.ds(start, size)], out_sems.at[i])
        copy.start()
        sent.append(copy)
    for copy in sent:
        copy.wait()


def combine(step, back, x, routes, logits, experts, capacity, tile=1024):
    slots, width = back.shape
    rows = x.shape[0]
    return pl.pallas_call(
        functools.partial(combine_kernel, step, experts, capacity, tile),
        in_specs=[ANY, ANY, VMEM, VMEM],
        out_specs=ANY,
        out_shape=jax.ShapeDtypeStruct((rows, width), jnp.bfloat16),
        scratch_shapes=[
            pltpu.VMEM((slots, width), jnp.bfloat16),
            pltpu.VMEM((rows, width), jnp.bfloat16),
            pltpu.VMEM((rows, width), jnp.bfloat16),
            pltpu.SemaphoreType.DMA((len(cuts(width, tile)) + 1,)),
            pltpu.SemaphoreType.DMA((len(cuts(width, tile)),)),
        ],
        compiler_params=PARAMS,
        cost_estimate=pl.CostEstimate(flops=4 * rows * slots * width, bytes_accessed=2 * (2 * rows + slots) * width, transcendentals=0),
        name="combine",
    )(back, x, routes, logits)
FIRST_PARTS = (896, 2688)
LAST_PARTS = (3584,)


def exchange(blocks, experts, capacity):
    width = blocks.shape[1]
    moved = lax.all_to_all(blocks.reshape(experts, capacity, width), "expert", 0, 0, tiled=True)
    return moved.reshape(experts * capacity, width)


def moved_from(value, odd):
    sections = lax.axis_size("section")
    return lax.ppermute(value, "section", [(i, (i + 1) % sections) for i in range(odd, sections, 2)])


def on_device(activations, norm_gain, w_gate, w_up, w_down, routes, gate_logits):
    experts = lax.axis_size("expert")
    start = activations[0]
    capacity = 2 * start.shape[0] * TOP // experts
    chosen, logits = (value[:, 0].transpose(0, 2, 1) for value in (routes, gate_logits))
    parity = lax.axis_index("section") % 2
    odd = parity == 1
    nothing = functools.partial(jnp.zeros_like, start)
    whole = (start.shape[1],)

    def in_turn(parts):
        rows = []
        for part in parts:
            if rows:
                part, rows[-1] = lax.optimization_barrier((part, rows[-1]))
            rows.append(exchange(part, experts, capacity))
        return rows

    def layer(step, current, packed, *after):
        produced = mlp(in_turn(packed), w_gate[0, 0], w_up[0, 0], w_down[0, 0], *after)
        back = exchange(produced, experts, capacity)
        return combine(step, back, current, chosen, logits, experts, capacity)

    def packed_rows(step, current, *kinds, flag=None):
        return pack(step, current, norm_gain, chosen, experts, capacity, *kinds, flag=flag)

    flag = parity.astype(jnp.int32).reshape(1)
    packed = packed_rows(0, start, whole, FIRST_PARTS, flag=flag)
    first_even = lax.cond(odd, nothing, lambda: layer(0, start, packed[:1]))
    near = moved_from(first_even, 0)
    first_odd = lax.cond(odd, lambda: layer(0, start, packed[1:], first_even), nothing)
    far = moved_from(first_odd, 1)
    early = lax.cond(odd, lambda: layer(1, near, packed_rows(1, near, whole)), nothing)
    far_out = moved_from(early, 1)
    late = lax.cond(odd, nothing, lambda: layer(1, far, packed_rows(1, far, LAST_PARTS), early))
    near_out = moved_from(late, 0)
    return lax.cond(odd, lambda: near_out, lambda: far_out)[None]


def solution(mesh):
    in_specs = (
        P("section", "expert", None),
        P("section", None),
        P("section", "expert", None, None),
        P("section", "expert", None, None),
        P("section", "expert", None, None),
        P(None, "section", "expert", None),
        P(None, "section", "expert", None),
    )
    return jax.shard_map(
        on_device, mesh=mesh, in_specs=in_specs, out_specs=P("section", "expert", None), check_vma=False
    )
```
